32 devices in a mesh: groups: 2 (over y), tp: 4 (over z), ad: 2 (over x), rep: 2 (over core).
Axes of the slice: x: 2, y: 2, z: 4, core: 2. Of those that a mesh axis runs over, the one named last changes fastest.
Arguments:
- tokens: bfloat16 [4096, 8192], P(('groups', 'ad', 'rep'), 'tp'), parts along dimension 0, may hold values from -6 to 6
- adapter_per_block: int32 [32], P(('groups', 'ad', 'rep')), parts along dimension 0, may hold values from 0 to 31, as said below
- placement: int32 [32], replicated, may hold values from 0 to 31, as said below
- weight: bfloat16 [8192, 4096], P('rep', 'tp'), may hold values from -0.0625 to 0.0625
- lowrank_down_weight: bfloat16 [32, 64, 8192], P('ad', None, 'tp'), may hold values from -0.0625 to 0.0625
- lowrank_up_weight: bfloat16 [32, 64, 4096], P('ad', None, 'tp'), may hold values from -0.75 to 0.75
Outputs:
- queries: bfloat16 [4096, 4096], P(('groups', 'ad', 'rep'), 'tp'), parts along dimension 0
The draws below stay inside these ranges and needn't reach their ends.
There are 2 independent parts, one for each index of `groups`. The reference program is written for one: setup_inputs(seed, part) draws one part's arguments, and reference() takes and returns one part's arrays. A program takes and returns all parts, laid end to end along the dimension named above; an argument that names none is the same for every part. Nothing has to cross between parts.
Inputs may be any that keep to these rules, and one draw needn't show every extreme that they name: Store row placement[a] lies on store shard a mod (2), shard k holding rows k * 16 to (k + 1) * 16 - 1; every store row is named once. `adapter_per_block`: of the 4 blocks of one device, at most 2 name adapters stored on one store shard, and in every draw some shard is named by exactly 2 blocks of some device. Adapters 0 and 31 are named in every draw.
All inputs are finite; a program needn't handle non-finite values.
Results may differ from the reference program's by a relative error of at most 0.0046.
Values may be sent and summed in bfloat16 or wider, within the bound.
A program may use at most 128 MiB of HBM per device.

```python
import jax
import jax.numpy as jnp
from jax import lax

MODEL_WIDTH = 8192
QUERY_FEATURES = 4096
ADAPTER_RANK = 64
BLOCK = 128
BLK_DEV = 4
SLOTS = 16
TOKEN_TOTAL = 2048
BLOCKS = 16
ADAPTER_COUNT = 32


def draw_placement(key, part):
    key = jax.random.fold_in(key, 11)
    owners = ADAPTER_COUNT // SLOTS
    key_list = jax.random.split(key, owners)
    orders = jax.vmap(lambda one_key: jax.random.permutation(one_key, SLOTS))(key_list)
    adapter = jnp.arange(ADAPTER_COUNT, dtype=jnp.int32)
    shard_of = adapter % owners
    within = adapter // owners
    return (shard_of * SLOTS + orders[shard_of, within]).astype(jnp.int32)


def draw_adapter_per_block(key, part):
    key = jax.random.fold_in(key, 23)
    owners = ADAPTER_COUNT // SLOTS
    per_owner = (BLK_DEV + owners - 1) // owners
    devices = BLOCKS // BLK_DEV
    owner_pool = jnp.tile(jnp.arange(owners, dtype=jnp.int32), per_owner)
    positions = jnp.arange(BLK_DEV, dtype=jnp.int32)

    def one_device(dev_key, device_number):
        key_order, key_left, key_right = jax.random.split(dev_key, 3)
        is_first = device_number == 0
        is_last = device_number == devices - 1
        target = jnp.where(is_last, 0, owners - 1).astype(jnp.int32)
        shuffled = jax.random.permutation(key_order, owner_pool)
        found = jnp.argmax((shuffled == target).astype(jnp.int32)).astype(jnp.int32)
        shuffled = shuffled.at[found].set(shuffled[0]).at[0].set(target)
        chosen = shuffled[:BLK_DEV]
        left_pick = jax.random.randint(key_left, (BLK_DEV,), 0, SLOTS)
        right_pick = jax.random.randint(key_right, (BLK_DEV,), 0, SLOTS)
        within = jnp.minimum(left_pick, right_pick)
        within = jnp.where((positions == 0) & is_first, SLOTS - 1, within)
        within = jnp.where((positions == 0) & is_last, 0, within)
        return (chosen + owners * within).astype(jnp.int32)
    device_numbers = jnp.arange(devices, dtype=jnp.int32)
    picked = jax.vmap(one_device)(jax.random.split(key, devices), device_numbers)
    return picked.reshape(BLOCKS).astype(jnp.int32)


def block_scale(key, shape, cuts, low, largest):
    gain = 1.0
    for axis_at, shards_of in cuts:
        draws = jax.random.uniform(jax.random.fold_in(jax.random.fold_in(key, 6), axis_at), (shards_of,), jnp.float32, low / len(cuts), largest / len(cuts))
        gain = gain * jnp.repeat(jnp.exp(draws), shape[axis_at] // shards_of).reshape((-1,) + (1,) * (len(shape) - 1 - axis_at))
    return gain


def normal_values(key, shape, width, bound, shards=(), kind=jnp.bfloat16):
    values = jax.random.normal(key, shape, jnp.float32) * width
    if len(shards) > 0:
        values = block_scale(key, shape, shards, -0.22, 0.18) * values
    return jnp.clip(values, min=-bound, max=bound).astype(kind)


def setup_inputs(seed: int = 0, part: int = 0) -> dict:
    seeds = jax.random.split(jax.random.key(seed), 7)
    part_keys = jax.random.split(jax.random.fold_in(seeds[6], part), 7)
    return {
        "tokens": normal_values(part_keys[0], (TOKEN_TOTAL, MODEL_WIDTH), 1.0, 6.0, ((0, 4), (1, 4))),
        "adapter_per_block": draw_adapter_per_block(jax.random.fold_in(jax.random.fold_in(seeds[6], part), 71), part),
        "placement": draw_placement(jax.random.fold_in(seeds[6], 71), part),
        "weight": normal_values(seeds[3], (MODEL_WIDTH, QUERY_FEATURES), MODEL_WIDTH ** -0.5, 0.0625, ((0, 2), (1, 4))),
        "lowrank_down_weight": normal_values(seeds[4], (ADAPTER_COUNT, ADAPTER_RANK, MODEL_WIDTH), MODEL_WIDTH ** -0.5, 0.0625, ((0, 2), (2, 4))),
        "lowrank_up_weight": normal_values(seeds[5], (ADAPTER_COUNT, ADAPTER_RANK, QUERY_FEATURES), ADAPTER_RANK ** -0.5, 0.75, ((0, 2), (2, 4))),
    }


lowrank_scale = 2.0


def reference(tokens, adapter_per_block, placement, weight, lowrank_down_weight, lowrank_up_weight):
    base_output = jnp.dot(tokens, weight, preferred_element_type=jnp.float32)
    store_row_index = placement[adapter_per_block]
    down_selected = lowrank_down_weight[store_row_index].astype(jnp.float32)
    up_selected = lowrank_up_weight[store_row_index].astype(jnp.float32)
    shaped = tokens.reshape(BLOCKS, BLOCK, MODEL_WIDTH).astype(jnp.float32)
    reduced_sum = jnp.einsum("bnd,brd->bnr", shaped, down_selected, precision=lax.Precision.HIGHEST).astype(jnp.bfloat16)
    lowrank_output = jnp.einsum("ajw,aws->ajs", reduced_sum.astype(jnp.float32), up_selected, precision=lax.Precision.HIGHEST)
    lowrank_output = lowrank_output.reshape(TOKEN_TOTAL, QUERY_FEATURES)
    return (base_output + lowrank_scale * lowrank_output).astype(jnp.bfloat16)
```

```python
import functools

import jax
import jax.numpy as jnp
from jax import lax
from jax.experimental import pallas as pl
from jax.experimental.pallas import tpu as pltpu
from jax.sharding import PartitionSpec as P

MESH = pl.DeviceIdType.MESH
lowrank_scale = 2.0
NT = (((1,), (1,)), ((), ()))


def remote(src, dst, send, recv, device):
    return pltpu.make_async_remote_copy(
        src_ref=src, dst_ref=dst, send_sem=send, recv_sem=recv, device_id=device, device_id_type=MESH
    )


def kernel(
    n, owners, block_count,
    pos, tok, wt, dpick, upick, out,
    g, w, acc, dn, up, part, pre, suf, snd_r, snd_l,
    local, tok_send, tok_recv, w_send, w_recv, a_send, a_recv, sum_send, sum_recv,
):
    z, a, r = lax.axis_index("tp"), lax.axis_index("ad"), lax.axis_index("rep")
    rows, feats = tok.shape
    half = wt.shape[0]
    size = rows // block_count
    per = dpick.shape[0] // owners
    has_left, has_right = z > 0, z < n - 1

    own_tok = pltpu.make_async_copy(tok, g.at[z], local.at[0])
    own_w = pltpu.make_async_copy(wt, w.at[pl.ds(r * half, half)], local.at[1])
    own_dn = pltpu.make_async_copy(dpick.at[pl.ds(a * per, per)], dn.at[pl.ds(a * per, per)], local.at[2])
    own_up = pltpu.make_async_copy(upick.at[pl.ds(a * per, per)], up.at[pl.ds(a * per, per)], local.at[3])
    own_tok.start()

    barrier = pltpu.get_barrier_semaphore()

    @pl.when(has_left)
    def _():
        pl.semaphore_signal(barrier, inc=1, device_id={"tp": z - 1}, device_id_type=MESH)

    @pl.when(has_right)
    def _():
        pl.semaphore_signal(barrier, inc=1, device_id={"tp": z + 1}, device_id_type=MESH)

    pl.semaphore_signal(barrier, inc=1, device_id={"rep": 1 - r}, device_id_type=MESH)
    for d in range(1, owners):
        pl.semaphore_signal(barrier, inc=1, device_id={"ad": lax.rem(a + d, owners)}, device_id_type=MESH)
    own_tok.wait()
    pl.semaphore_wait(
        barrier, owners + jnp.where(has_left, 1, 0) + jnp.where(has_right, 1, 0)
    )

    def piece(shard, c):
        return g.at[shard, pl.ds(pl.multiple_of(c * size, size), size)]

    def to_right(h, c):
        return remote(piece(z - h, c), piece(z - h, c), tok_send.at[0, h, c], tok_recv.at[0, h, c], {"tp": z + 1})

    def to_left(h, c):
        return remote(piece(z + h, c), piece(z + h, c), tok_send.at[1, h, c], tok_recv.at[1, h, c], {"tp": z - 1})

    def from_left(h, c):
        return remote(piece(z - 1 - h, c), piece(z - 1 - h, c), tok_send.at[0, h, c], tok_recv.at[0, h, c], {"tp": z - 1})

    def from_right(h, c):
        return remote(piece(z + 1 + h, c), piece(z + 1 + h, c), tok_send.at[1, h, c], tok_recv.at[1, h, c], {"tp": z + 1})

    def first(c, _):
        @pl.when(has_left)
        def _():
            to_left(0, c).start()

        @pl.when(has_right)
        def _():
            to_right(0, c).start()

        return 0

    lax.fori_loop(0, block_count, first, 0)

    give_w = remote(wt, w.at[pl.ds(r * half, half)], w_send, w_recv, {"rep": 1 - r})
    take_w = remote(wt, w.at[pl.ds((1 - r) * half, half)], w_send, w_recv, {"rep": 1 - r})
    give_w.start()
    own_w.start()
    own_dn.start()
    own_up.start()
    gives, takes = [], []
    for d in range(1, owners):
        to, frm = lax.rem(a + d, owners), lax.rem(a + owners - d, owners)
        for k, (pick, store) in enumerate(((dpick, dn), (upick, up))):
            gives.append(remote(
                pick.at[pl.ds(to * per, per)], store.at[pl.ds(a * per, per)],
                a_send.at[k, d - 1], a_recv.at[k, d - 1], {"ad": to},
            ))
            takes.append(remote(
                pick.at[pl.ds(to * per, per)], store.at[pl.ds(frm * per, per)],
                a_send.at[k, d - 1], a_recv.at[k, d - 1], {"ad": frm},
            ))
            gives[-1].start()

    @pl.when(z == 0)
    def _():
        pre[...] = jnp.zeros_like(pre)

    @pl.when(z == n - 1)
    def _():
        suf[...] = jnp.zeros_like(suf)

    def product(shard, c):
        at = pl.ds(pl.multiple_of(c * size, size), size)
        return jnp.dot(
            g[shard, at, :], w[pl.ds(pl.multiple_of(shard * feats, feats), feats), :],
            preferred_element_type=jnp.float32,
        )

    own_w.wait()
    take_w.wait_recv()

    def own(c, _):
        acc[pl.ds(pl.multiple_of(c * size, size), size), :] = product(z, c)
        return 0

    lax.fori_loop(0, block_count, own, 0)

    own_dn.wait()
    own_up.wait()
    for take in takes:
        take.wait_recv()
    for b in range(block_count):
        part[b] = lax.dot_general(
            dn[pos[b]], g[z, pl.ds(b * size, size), :], NT, preferred_element_type=jnp.float32
        )

    sum_right = remote(snd_r, pre, sum_send.at[0], sum_recv.at[0], {"tp": z + 1})
    sum_left = remote(snd_l, suf, sum_send.at[1], sum_recv.at[1], {"tp": z - 1})

    def hop(h, _):
        def chunk(c, _):
            @pl.when(z - 1 - h >= 0)
            def _():
                from_left(h, c).wait_recv()

                @pl.when(has_right)
                def _():
                    to_right(h + 1, c).start()

            @pl.when(z + 1 + h <= n - 1)
            def _():
                from_right(h, c).wait_recv()

                @pl.when(has_left)
                def _():
                    to_left(h + 1, c).start()

            at = pl.ds(pl.multiple_of(c * size, size), size)

            @pl.when(z - 1 - h >= 0)
            def _():
                acc[at, :] += product(z - 1 - h, c)

            @pl.when(z + 1 + h <= n - 1)
            def _():
                acc[at, :] += product(z + 1 + h, c)

            return 0

        lax.fori_loop(0, block_count, chunk, 0)

        @pl.when((z == h) & has_right)
        def _():
            @pl.when(has_left)
            def _():
                sum_right.wait_recv()

            snd_r[...] = part[...] + pre[...]
            sum_right.start()

        @pl.when((n - 1 - z == h) & has_left)
        def _():
            @pl.when(has_right)
            def _():
                sum_left.wait_recv()

            snd_l[...] = part[...] + suf[...]
            sum_left.start()

        return 0

    lax.fori_loop(0, n - 1, hop, 0)

    @pl.when(z == n - 1)
    def _():
        sum_right.wait_recv()

    @pl.when(z == 0)
    def _():
        sum_left.wait_recv()

    for b in range(block_count):
        at = pl.ds(b * size, size)
        reduced = jnp.transpose(part[b] + pre[b] + suf[b]).astype(jnp.bfloat16)
        lora = jnp.dot(reduced, up[pos[b]], preferred_element_type=jnp.float32)
        out[at, :] = (acc[at, :] + lowrank_scale * lora).astype(jnp.bfloat16)

    def sent(h, _):
        def chunk(c, _):
            @pl.when(has_right & (z - h >= 0))
            def _():
                to_right(h, c).wait_send()

            @pl.when(has_left & (z + h <= n - 1))
            def _():
                to_left(h, c).wait_send()

            return 0

        lax.fori_loop(0, block_count, chunk, 0)
        return 0

    lax.fori_loop(0, n - 1, sent, 0)
    give_w.wait_send()
    for give in gives:
        give.wait_send()

    @pl.when(has_right)
    def _():
        sum_right.wait_send()

    @pl.when(has_left)
    def _():
        sum_left.wait_send()


def body(mesh, tokens, adapter_per_block, placement, weight, lowrank_down_weight, lowrank_up_weight):
    rows, feats = tokens.shape
    block_count = adapter_per_block.shape[0]
    size = rows // block_count
    slots, rank, _ = lowrank_down_weight.shape
    half, columns = weight.shape
    n, owners = mesh.shape["tp"], mesh.shape["ad"]
    per_owner = (block_count + owners - 1) // owners
    table = jnp.arange(placement.shape[0], dtype=jnp.int32)
    store_row = jnp.sum(
        jnp.where(adapter_per_block[:, None] == table[None, :], placement[None, :], 0), axis=1
    )
    owner_of = store_row // slots
    slot_of = store_row % slots
    index = jnp.arange(block_count, dtype=jnp.int32)
    earlier = (owner_of[:, None] == owner_of[None, :]) & (index[None, :] < index[:, None])
    position = owner_of * per_owner + jnp.sum(earlier.astype(jnp.int32), axis=1)
    places = jnp.arange(owners * per_owner, dtype=jnp.int32)
    asks = jnp.sum(jnp.where(position[None, :] == places[:, None], slot_of[None, :], 0), axis=1)
    asked = lax.all_to_all(
        asks.reshape(owners, per_owner), "ad", split_axis=0, concat_axis=0, tiled=True
    ).reshape(-1)
    down_pick = jnp.take(lowrank_down_weight, asked, axis=0, mode="clip")
    up_pick = jnp.take(lowrank_up_weight, asked, axis=0, mode="clip")
    total = owners * per_owner
    bf16, f32 = jnp.bfloat16, jnp.float32
    sums = pltpu.VMEM((block_count, rank, size), f32)
    anyspace = pl.BlockSpec(memory_space=pl.ANY)
    peers = max(owners - 1, 1)
    return pl.pallas_call(
        functools.partial(kernel, n, owners, block_count),
        out_shape=jax.ShapeDtypeStruct((rows, columns), bf16),
        in_specs=[pl.BlockSpec(memory_space=pltpu.SMEM)] + [anyspace] * 4,
        out_specs=pl.BlockSpec(memory_space=pltpu.VMEM),
        scratch_shapes=[
            pltpu.VMEM((n, rows, feats), bf16),
            pltpu.VMEM((2 * half, columns), bf16),
            pltpu.VMEM((rows, columns), f32),
            pltpu.VMEM((total, rank, feats), bf16),
            pltpu.VMEM((total, rank, columns), bf16),
            sums, sums, sums, sums, sums,
            pltpu.SemaphoreType.DMA((4,)),
            pltpu.SemaphoreType.DMA((2, n - 1, block_count)),
            pltpu.SemaphoreType.DMA((2, n - 1, block_count)),
            pltpu.SemaphoreType.DMA,
            pltpu.SemaphoreType.DMA,
            pltpu.SemaphoreType.DMA((2, peers)),
            pltpu.SemaphoreType.DMA((2, peers)),
            pltpu.SemaphoreType.DMA((2,)),
            pltpu.SemaphoreType.DMA((2,)),
        ],
        compiler_params=pltpu.CompilerParams(
            collective_id=0, has_side_effects=True, vmem_limit_bytes=52 * 1024 * 1024
        ),
        cost_estimate=pl.CostEstimate(
            flops=4 * rows * half * columns, bytes_accessed=4 * half * columns, transcendentals=0
        ),
    )(position, tokens, weight, down_pick, up_pick)


def solution(mesh):
    return jax.shard_map(
        functools.partial(body, mesh),
        mesh=mesh,
        in_specs=(
            P(("groups", "ad", "rep"), "tp"),
            P(("groups", "ad", "rep")),
            P(),
            P("rep", "tp"),
            P("ad", None, "tp"),
            P("ad", None, "tp"),
        ),
        out_specs=P(("groups", "ad", "rep"), "tp"),
        check_vma=False,
    )
```

```python
import functools

import jax
import jax.numpy as jnp
from jax import lax
from jax.experimental import pallas as pl
from jax.experimental.pallas import tpu as pltpu
from jax.sharding import PartitionSpec as P

MESH = pl.DeviceIdType.MESH
lowrank_scale = 2.0
NT = (((1,), (1,)), ((), ()))


def remote(src, dst, send, recv, device):
    return pltpu.make_async_remote_copy(
        src_ref=src, dst_ref=dst, send_sem=send, recv_sem=recv, device_id=device, device_id_type=MESH
    )


def kernel(
    n, owners, block_count,
    pos, tok, wt, dpick, upick, out,
    g, w, acc, dn, up, part, pre, suf, snd_r, snd_l, wx, far_sum, aid_out, aid_in,
    local, tok_send, tok_recv, w_send, w_recv, a_send, a_recv, sum_send, sum_recv,
    gv_send, gv_recv, x_send, x_recv, p_send, p_recv, aid_send, aid_recv,
):
    z, a, r = lax.axis_index("tp"), lax.axis_index("ad"), lax.axis_index("rep")
    rows, feats = tok.shape
    half = wt.shape[0]
    size = rows // block_count
    per = dpick.shape[0] // owners
    has_left, has_right = z > 0, z < n - 1
    mid = n // 2
    first_end, last_end, by_first, by_last = z == 0, z == n - 1, z == 1, z == n - 2
    end, helper = first_end | last_end, by_first | by_last
    end_of, helper_of = jnp.where(by_first, 0, n - 1), jnp.where(first_end, 1, n - 2)
    giver = (first_end & (r == 1)) | (last_end & (r == 0))
    sub = half // (2 * owners * block_count)

    own_tok = pltpu.make_async_copy(tok, g.at[z], local.at[0])
    own_w = pltpu.make_async_copy(wt, w.at[pl.ds(r * half, half)], local.at[1])
    own_dn = pltpu.make_async_copy(dpick.at[pl.ds(a * per, per)], dn.at[pl.ds(a * per, per)], local.at[2])
    own_up = pltpu.make_async_copy(upick.at[pl.ds(a * per, per)], up.at[pl.ds(a * per, per)], local.at[3])
    own_tok.start()

    barrier = pltpu.get_barrier_semaphore()

    @pl.when(has_left)
    def _():
        for core in range(2):
            pl.semaphore_signal(barrier, inc=1, device_id={"tp": z - 1, "rep": core}, device_id_type=MESH)

    @pl.when(has_right)
    def _():
        for core in range(2):
            pl.semaphore_signal(barrier, inc=1, device_id={"tp": z + 1, "rep": core}, device_id_type=MESH)

    pl.semaphore_signal(barrier, inc=1, device_id={"rep": 1 - r}, device_id_type=MESH)
    for d in range(1, owners):
        pl.semaphore_signal(barrier, inc=1, device_id={"ad": lax.rem(a + d, owners)}, device_id_type=MESH)
    own_tok.wait()
    pl.semaphore_wait(
        barrier, owners + jnp.where(has_left, 2, 0) + jnp.where(has_right, 2, 0)
    )

    def piece(shard, c):
        return g.at[shard, pl.ds(pl.multiple_of(c * size, size), size)]

    def to_right(h, c):
        return remote(piece(z - h, c), piece(z - h, c), tok_send.at[0, h, c], tok_recv.at[0, h, c], {"tp": z + 1})

    def to_left(h, c):
        return remote(piece(z + h, c), piece(z + h, c), tok_send.at[1, h, c], tok_recv.at[1, h, c], {"tp": z - 1})

    def from_left(h, c):
        return remote(piece(z - 1 - h, c), piece(z - 1 - h, c), tok_send.at[0, h, c], tok_recv.at[0, h, c], {"tp": z - 1})

    def from_right(h, c):
        return remote(piece(z + 1 + h, c), piece(z + 1 + h, c), tok_send.at[1, h, c], tok_recv.at[1, h, c], {"tp": z + 1})

    def share(owner, core, j):
        return pl.ds(pl.multiple_of(((owner * 2 + core) * block_count + j) * sub, sub), sub)

    def give(core, j):
        at = share(a, core, j)
        return remote(wt.at[at], wx.at[at], gv_send.at[core, j], gv_recv.at[j], {"tp": helper_of, "rep": core})

    def given(j):
        at = share(a, r, j)
        return remote(wt.at[at], wx.at[at], gv_send.at[0, j], gv_recv.at[j], {"tp": end_of})

    def across(d, j):
        at = wx.at[share(a, r, j)]
        return remote(at, at, x_send.at[d - 1, j], x_recv.at[d - 1, j], {"ad": lax.rem(a + d, owners)})

    def from_across(d, j):
        at = wx.at[share(lax.rem(a + owners - d, owners), r, j)]
        return remote(at, at, x_send.at[d - 1, j], x_recv.at[d - 1, j], {"ad": lax.rem(a + owners - d, owners)})

    def beside(d, core, j):
        at = wx.at[share(lax.rem(a + owners - d, owners), core, j)]
        return remote(at, at, p_send.at[d, j], p_recv.at[d, j], {"rep": 1 - r})

    def aid(c, device):
        at = pl.ds(pl.multiple_of(c * size, size), size)
        return remote(aid_out.at[at], aid_in.at[at], aid_send.at[c], aid_recv.at[c], {"tp": device})

    @pl.when(giver)
    def _():
        def start(j, _):
            for core in range(2):
                give(core, j).start()
            return 0

        lax.fori_loop(0, block_count, start, 0)

    def first(c, _):
        @pl.when(has_left & jnp.logical_not(last_end))
        def _():
            to_left(0, c).start()

        @pl.when(has_right & jnp.logical_not(first_end))
        def _():
            to_right(0, c).start()

        return 0

    lax.fori_loop(0, block_count, first, 0)

    give_w = remote(wt, w.at[pl.ds(r * half, half)], w_send, w_recv, {"rep": 1 - r})
    take_w = remote(wt, w.at[pl.ds((1 - r) * half, half)], w_send, w_recv, {"rep": 1 - r})
    give_w.start()
    own_w.start()
    own_dn.start()
    own_up.start()
    gives, takes = [], []
    for d in range(1, owners):
        to, frm = lax.rem(a + d, owners), lax.rem(a + owners - d, owners)
        for k, (pick, store) in enumerate(((dpick, dn), (upick, up))):
            gives.append(remote(
                pick.at[pl.ds(to * per, per)], store.at[pl.ds(a * per, per)],
                a_send.at[k, d - 1], a_recv.at[k, d - 1], {"ad": to},
            ))
            takes.append(remote(
                pick.at[pl.ds(to * per, per)], store.at[pl.ds(frm * per, per)],
                a_send.at[k, d - 1], a_recv.at[k, d - 1], {"ad": frm},
            ))
            gives[-1].start()

    @pl.when(z == 0)
    def _():
        pre[...] = jnp.zeros_like(pre)

    @pl.when(z == n - 1)
    def _():
        suf[...] = jnp.zeros_like(suf)

    def product(shard, c):
        at = pl.ds(pl.multiple_of(c * size, size), size)
        return jnp.dot(
            g[shard, at, :], w[pl.ds(pl.multiple_of(shard * feats, feats), feats), :],
            preferred_element_type=jnp.float32,
        )

    own_w.wait()
    take_w.wait_recv()

    def own(c, _):
        acc[pl.ds(pl.multiple_of(c * size, size), size), :] = product(z, c)
        return 0

    lax.fori_loop(0, block_count, own, 0)

    own_dn.wait()
    own_up.wait()
    for take in takes:
        take.wait_recv()
    for b in range(block_count):
        part[b] = lax.dot_general(
            dn[pos[b]], g[z, pl.ds(b * size, size), :], NT, preferred_element_type=jnp.float32
        )

    sum_right = remote(snd_r, pre, sum_send.at[0], sum_recv.at[0], {"tp": z + 1})
    sum_left = remote(snd_l, suf, sum_send.at[1], sum_recv.at[1], {"tp": z - 1})

    def hop(h, _):
        hr = h - jnp.where(by_first, 1, 0)
        hl = h - jnp.where(by_last, 1, 0)
        left_shard, right_shard = z - 1 - hr, z + 1 + hl
        takes_left = (hr >= 0) & (left_shard >= 0) & jnp.logical_not(last_end & (left_shard < mid))
        takes_right = (hl >= 0) & (right_shard <= n - 1) & jnp.logical_not(first_end & (right_shard >= mid))

        def chunk(c, _):
            @pl.when(takes_left)
            def _():
                from_left(hr, c).wait_recv()

                @pl.when(has_right & jnp.logical_not(by_last & (left_shard < mid)))
                def _():
                    to_right(hr + 1, c).start()

            @pl.when(takes_right)
            def _():
                from_right(hl, c).wait_recv()

                @pl.when(has_left & jnp.logical_not(by_first & (right_shard >= mid)))
                def _():
                    to_left(hl + 1, c).start()

            @pl.when(end & (h == 0) & (c == block_count - 1))
            def _():
                def late(k, _):
                    @pl.when(first_end)
                    def _():
                        to_right(0, k).start()

                    @pl.when(last_end)
                    def _():
                        to_left(0, k).start()

                    return 0

                lax.fori_loop(0, block_count, late, 0)

            @pl.when(helper & (h == 0))
            def _():
                given(c).wait_recv()
                for d in range(1, owners):
                    across(d, c).start()
                beside(0, r, c).start()

            @pl.when(helper & (h * block_count + c >= 1) & (h * block_count + c <= block_count))
            def _():
                for d in range(1, owners):
                    from_across(d, h * block_count + c - 1).wait_recv()
                    beside(d, r, h * block_count + c - 1).start()

            at = pl.ds(pl.multiple_of(c * size, size), size)

            @pl.when(takes_left)
            def _():
                acc[at, :] += product(left_shard, c)

            @pl.when(takes_right)
            def _():
                acc[at, :] += product(right_shard, c)

            @pl.when(helper & (h == n - 3))
            def _():
                @pl.when(c == 0)
                def _():
                    def arrived(j, _):
                        for d in range(owners):
                            beside(d, 1 - r, j).wait_recv()
                        return 0

                    lax.fori_loop(0, block_count, arrived, 0)

                base = jnp.where(by_first, mid, 0)
                far_sum[...] = jnp.zeros_like(far_sum)

                def far(k, _):
                    far_sum[...] += jnp.dot(
                        g[base + k, at, :], wx[pl.ds(pl.multiple_of(k * feats, feats), feats), :],
                        preferred_element_type=jnp.float32,
                    )
                    return 0

                lax.fori_loop(0, n - mid, far, 0)
                aid_out[at, :] = far_sum[...].astype(jnp.bfloat16)
                aid(c, end_of).start()

            return 0

        lax.fori_loop(0, block_count, chunk, 0)

        @pl.when((z == h) & has_right)
        def _():
            @pl.when(has_left)
            def _():
                sum_right.wait_recv()

            snd_r[...] = part[...] + pre[...]
            sum_right.start()

        @pl.when((n - 1 - z == h) & has_left)
        def _():
            @pl.when(has_right)
            def _():
                sum_left.wait_recv()

            snd_l[...] = part[...] + suf[...]
            sum_left.start()

        return 0

    lax.fori_loop(0, n - 1, hop, 0)

    @pl.when(z == n - 1)
    def _():
        sum_right.wait_recv()

    @pl.when(z == 0)
    def _():
        sum_left.wait_recv()

    for b in range(block_count):
        at = pl.ds(b * size, size)
        reduced = jnp.transpose(part[b] + pre[b] + suf[b]).astype(jnp.bfloat16)
        lora = jnp.dot(reduced, up[pos[b]], preferred_element_type=jnp.float32)

        @pl.when(end)
        def _():
            aid(b, helper_of).wait_recv()
            acc[at, :] += aid_in[at, :].astype(jnp.float32)

        out[at, :] = (acc[at, :] + lowrank_scale * lora).astype(jnp.bfloat16)

    def sent(h, _):
        def chunk(c, _):
            @pl.when(has_right & (z - h >= 0) & jnp.logical_not(by_last & (z - h < mid)))
            def _():
                to_right(h, c).wait_send()

            @pl.when(has_left & (z + h <= n - 1) & jnp.logical_not(by_first & (z + h >= mid)))
            def _():
                to_left(h, c).wait_send()

            return 0

        lax.fori_loop(0, block_count, chunk, 0)
        return 0

    lax.fori_loop(0, n - 1, sent, 0)
    give_w.wait_send()
    for gift in gives:
        gift.wait_send()

    def done(j, _):
        @pl.when(giver)
        def _():
            for core in range(2):
                give(core, j).wait_send()

        @pl.when(helper)
        def _():
            for d in range(1, owners):
                across(d, j).wait_send()
            for d in range(owners):
                beside(d, r, j).wait_send()
            aid(j, end_of).wait_send()

        return 0

    lax.fori_loop(0, block_count, done, 0)

    @pl.when(has_right)
    def _():
        sum_right.wait_send()

    @pl.when(has_left)
    def _():
        sum_left.wait_send()


def body(mesh, tokens, adapter_per_block, placement, weight, lowrank_down_weight, lowrank_up_weight):
    rows, feats = tokens.shape
    block_count = adapter_per_block.shape[0]
    size = rows // block_count
    slots, rank, _ = lowrank_down_weight.shape
    half, columns = weight.shape
    n, owners = mesh.shape["tp"], mesh.shape["ad"]
    per_owner = (block_count + owners - 1) // owners
    table = jnp.arange(placement.shape[0], dtype=jnp.int32)
    store_row = jnp.sum(
        jnp.where(adapter_per_block[:, None] == table[None, :], placement[None, :], 0), axis=1
    )
    owner_of = store_row // slots
    slot_of = store_row % slots
    index = jnp.arange(block_count, dtype=jnp.int32)
    earlier = (owner_of[:, None] == owner_of[None, :]) & (index[None, :] < index[:, None])
    position = owner_of * per_owner + jnp.sum(earlier.astype(jnp.int32), axis=1)
    places = jnp.arange(owners * per_owner, dtype=jnp.int32)
    asks = jnp.sum(jnp.where(position[None, :] == places[:, None], slot_of[None, :], 0), axis=1)
    asked = lax.all_to_all(
        asks.reshape(owners, per_owner), "ad", split_axis=0, concat_axis=0, tiled=True
    ).reshape(-1)
    down_pick = jnp.take(lowrank_down_weight, asked, axis=0, mode="clip")
    up_pick = jnp.take(lowrank_up_weight, asked, axis=0, mode="clip")
    total = owners * per_owner
    bf16, f32 = jnp.bfloat16, jnp.float32
    sums = pltpu.VMEM((block_count, rank, size), f32)
    anyspace = pl.BlockSpec(memory_space=pl.ANY)
    peers = max(owners - 1, 1)
    return pl.pallas_call(
        functools.partial(kernel, n, owners, block_count),
        out_shape=jax.ShapeDtypeStruct((rows, columns), bf16),
        in_specs=[pl.BlockSpec(memory_space=pltpu.SMEM)] + [anyspace] * 4,
        out_specs=pl.BlockSpec(memory_space=pltpu.VMEM),
        scratch_shapes=[
            pltpu.VMEM((n, rows, feats), bf16),
            pltpu.VMEM((2 * half, columns), bf16),
            pltpu.VMEM((rows, columns), f32),
            pltpu.VMEM((total, rank, feats), bf16),
            pltpu.VMEM((total, rank, columns), bf16),
            sums, sums, sums, sums, sums,
            pltpu.VMEM((half, columns), bf16),
            pltpu.VMEM((size, columns), f32),
            pltpu.VMEM((rows, columns), bf16),
            pltpu.VMEM((rows, columns), bf16),
            pltpu.SemaphoreType.DMA((4,)),
            pltpu.SemaphoreType.DMA((2, n - 1, block_count)),
            pltpu.SemaphoreType.DMA((2, n - 1, block_count)),
            pltpu.SemaphoreType.DMA,
            pltpu.SemaphoreType.DMA,
            pltpu.SemaphoreType.DMA((2, peers)),
            pltpu.SemaphoreType.DMA((2, peers)),
            pltpu.SemaphoreType.DMA((2,)),
            pltpu.SemaphoreType.DMA((2,)),
            pltpu.SemaphoreType.DMA((2, block_count)),
            pltpu.SemaphoreType.DMA((block_count,)),
            pltpu.SemaphoreType.DMA((peers, block_count)),
            pltpu.SemaphoreType.DMA((peers, block_count)),
            pltpu.SemaphoreType.DMA((owners, block_count)),
            pltpu.SemaphoreType.DMA((owners, block_count)),
            pltpu.SemaphoreType.DMA((block_count,)),
            pltpu.SemaphoreType.DMA((block_count,)),
        ],
        compiler_params=pltpu.CompilerParams(
            collective_id=0, has_side_effects=True, vmem_limit_bytes=56 * 1024 * 1024
        ),
        cost_estimate=pl.CostEstimate(
            flops=4 * rows * half * columns, bytes_accessed=4 * half * columns, transcendentals=0
        ),
    )(position, tokens, weight, down_pick, up_pick)


def solution(mesh):
    return jax.shard_map(
        functools.partial(body, mesh),
        mesh=mesh,
        in_specs=(
            P(("groups", "ad", "rep"), "tp"),
            P(("groups", "ad", "rep")),
            P(),
            P("rep", "tp"),
            P("ad", None, "tp"),
            P("ad", None, "tp"),
        ),
        out_specs=P(("groups", "ad", "rep"), "tp"),
        check_vma=False,
    )
```

```python
import functools

import jax
import jax.numpy as jnp
from jax import lax
from jax.experimental import pallas as pl
from jax.experimental.pallas import tpu as pltpu
from jax.sharding import PartitionSpec as P

MESH = pl.DeviceIdType.MESH
lowrank_scale = 2.0
NT = (((1,), (1,)), ((), ()))


def remote(src, dst, send, recv, device):
    return pltpu.make_async_remote_copy(
        src_ref=src, dst_ref=dst, send_sem=send, recv_sem=recv, device_id=device, device_id_type=MESH
    )


def kernel(
    n, owners, block_count,
    pos, tok, wt, dpick, upick, out,
    g, w, acc, dn, up, part, pre, suf, snd_r, snd_l, wx, far_sum, aid_out, aid_in,
    local, tok_send, tok_recv, w_send, w_recv, a_send, a_recv, sum_send, sum_recv,
    gv_send, gv_recv, x_send, x_recv, p_send, p_recv, aid_send, aid_recv,
):
    z, a, r = lax.axis_index("tp"), lax.axis_index("ad"), lax.axis_index("rep")
    rows, feats = tok.shape
    half = wt.shape[0]
    size = rows // block_count
    per = dpick.shape[0] // owners
    has_left, has_right = z > 0, z < n - 1
    mid = n // 2
    first_end, last_end, by_first, by_last = z == 0, z == n - 1, z == 1, z == n - 2
    end, helper = first_end | last_end, by_first | by_last
    end_of, helper_of = jnp.where(by_first, 0, n - 1), jnp.where(first_end, 1, n - 2)
    giver = (first_end & (r == 1)) | (last_end & (r == 0))
    sub = half // (2 * owners * block_count)

    own_tok = pltpu.make_async_copy(tok, g.at[z], local.at[0])
    own_w = pltpu.make_async_copy(wt, w.at[pl.ds(r * half, half)], local.at[1])
    own_dn = pltpu.make_async_copy(dpick.at[pl.ds(a * per, per)], dn.at[pl.ds(a * per, per)], local.at[2])
    own_up = pltpu.make_async_copy(upick.at[pl.ds(a * per, per)], up.at[pl.ds(a * per, per)], local.at[3])
    own_tok.start()

    barrier = pltpu.get_barrier_semaphore()

    @pl.when(has_left)
    def _():
        for core in range(2):
            pl.semaphore_signal(barrier, inc=1, device_id={"tp": z - 1, "rep": core}, device_id_type=MESH)

    @pl.when(has_right)
    def _():
        for core in range(2):
            pl.semaphore_signal(barrier, inc=1, device_id={"tp": z + 1, "rep": core}, device_id_type=MESH)

    pl.semaphore_signal(barrier, inc=1, device_id={"rep": 1 - r}, device_id_type=MESH)
    for d in range(1, owners):
        pl.semaphore_signal(barrier, inc=1, device_id={"ad": lax.rem(a + d, owners)}, device_id_type=MESH)
    own_tok.wait()
    pl.semaphore_wait(
        barrier, owners + jnp.where(has_left, 2, 0) + jnp.where(has_right, 2, 0)
    )

    def piece(shard, c):
        return g.at[shard, pl.ds(pl.multiple_of(c * size, size), size)]

    def to_right(h, c):
        return remote(piece(z - h, c), piece(z - h, c), tok_send.at[0, h, c], tok_recv.at[0, h, c], {"tp": z + 1})

    def to_left(h, c):
        return remote(piece(z + h, c), piece(z + h, c), tok_send.at[1, h, c], tok_recv.at[1, h, c], {"tp": z - 1})

    def from_left(h, c):
        return remote(piece(z - 1 - h, c), piece(z - 1 - h, c), tok_send.at[0, h, c], tok_recv.at[0, h, c], {"tp": z - 1})

    def from_right(h, c):
        return remote(piece(z + 1 + h, c), piece(z + 1 + h, c), tok_send.at[1, h, c], tok_recv.at[1, h, c], {"tp": z + 1})

    def share(owner, core, j):
        return pl.ds(pl.multiple_of(((owner * 2 + core) * block_count + j) * sub, sub), sub)

    def give(core, j):
        at = share(a, core, j)
        return remote(wt.at[at], wx.at[at], gv_send.at[core, j], gv_recv.at[j], {"tp": helper_of, "rep": core})

    def given(j):
        at = share(a, r, j)
        return remote(wt.at[at], wx.at[at], gv_send.at[0, j], gv_recv.at[j], {"tp": end_of})

    def across(d, j):
        at = wx.at[share(a, r, j)]
        return remote(at, at, x_send.at[d - 1, j], x_recv.at[d - 1, j], {"ad": lax.rem(a + d, owners)})

    def from_across(d, j):
        at = wx.at[share(lax.rem(a + owners - d, owners), r, j)]
        return remote(at, at, x_send.at[d - 1, j], x_recv.at[d - 1, j], {"ad": lax.rem(a + owners - d, owners)})

    def beside(d, core, j):
        at = wx.at[share(lax.rem(a + owners - d, owners), core, j)]
        return remote(at, at, p_send.at[d, j], p_recv.at[d, j], {"rep": 1 - r})

    def aid(c, device):
        at = pl.ds(pl.multiple_of(c * size, size), size)
        return remote(aid_out.at[at], aid_in.at[at], aid_send.at[c], aid_recv.at[c], {"tp": device})

    @pl.when(giver)
    def _():
        def start(j, _):
            for core in range(2):
                give(core, j).start()
            return 0

        lax.fori_loop(0, block_count, start, 0)

    def first(c, _):
        @pl.when(has_left & jnp.logical_not(last_end))
        def _():
            to_left(0, c).start()

        @pl.when(has_right & jnp.logical_not(first_end))
        def _():
            to_right(0, c).start()

        return 0

    lax.fori_loop(0, block_count, first, 0)

    give_w = remote(wt, w.at[pl.ds(r * half, half)], w_send, w_recv, {"rep": 1 - r})
    take_w = remote(wt, w.at[pl.ds((1 - r) * half, half)], w_send, w_recv, {"rep": 1 - r})
    give_w.start()
    own_w.start()
    own_dn.start()
    own_up.start()
    gives, takes = [], []
    for d in range(1, owners):
        to, frm = lax.rem(a + d, owners), lax.rem(a + owners - d, owners)
        for k, (pick, store) in enumerate(((dpick, dn), (upick, up))):
            gives.append(remote(
                pick.at[pl.ds(to * per, per)], store.at[pl.ds(a * per, per)],
                a_send.at[k, d - 1], a_recv.at[k, d - 1], {"ad": to},
            ))
            takes.append(remote(
                pick.at[pl.ds(to * per, per)], store.at[pl.ds(frm * per, per)],
                a_send.at[k, d - 1], a_recv.at[k, d - 1], {"ad": frm},
            ))
            gives[-1].start()

    @pl.when(z == 0)
    def _():
        pre[...] = jnp.zeros_like(pre)

    @pl.when(z == n - 1)
    def _():
        suf[...] = jnp.zeros_like(suf)

    def product(shard, c):
        at = pl.ds(pl.multiple_of(c * size, size), size)
        return jnp.dot(
            g[shard, at, :], w[pl.ds(pl.multiple_of(shard * feats, feats), feats), :],
            preferred_element_type=jnp.float32,
        )

    own_w.wait()
    take_w.wait_recv()

    def own(c, _):
        acc[pl.ds(pl.multiple_of(c * size, size), size), :] = product(z, c)
        return 0

    lax.fori_loop(0, block_count, own, 0)

    own_dn.wait()
    own_up.wait()
    for take in takes:
        take.wait_recv()
    for b in range(block_count):
        part[b] = lax.dot_general(
            dn[pos[b]], g[z, pl.ds(b * size, size), :], NT, preferred_element_type=jnp.float32
        )

    sum_right = remote(snd_r, pre, sum_send.at[0], sum_recv.at[0], {"tp": z + 1})
    sum_left = remote(snd_l, suf, sum_send.at[1], sum_recv.at[1], {"tp": z - 1})

    def hop(h, _):
        hr = h - jnp.where(by_first, 1, 0)
        hl = h - jnp.where(by_last, 1, 0)
        left_shard, right_shard = z - 1 - hr, z + 1 + hl
        takes_left = (hr >= 0) & (left_shard >= 0) & jnp.logical_not(last_end & (left_shard < mid))
        takes_right = (hl >= 0) & (right_shard <= n - 1) & jnp.logical_not(first_end & (right_shard >= mid))

        def pass_right(c, _=0):
            from_left(hr, c).wait_recv()

            @pl.when(has_right & jnp.logical_not(by_last & (left_shard < mid)))
            def _():
                to_right(hr + 1, c).start()

            return 0

        def pass_left(c, _=0):
            from_right(hl, c).wait_recv()

            @pl.when(has_left & jnp.logical_not(by_first & (right_shard >= mid)))
            def _():
                to_left(hl + 1, c).start()

            return 0

        def chunk(c, _):
            low = jnp.where(c == 0, 0, c + 1)
            high = jnp.where(c + 2 < block_count, c + 2, block_count)

            @pl.when(takes_left & by_first)
            def _():
                lax.fori_loop(low, high, pass_right, 0)

            @pl.when(takes_right & by_last)
            def _():
                lax.fori_loop(low, high, pass_left, 0)

            @pl.when(takes_left & jnp.logical_not(by_first))
            def _():
                pass_right(c)

            @pl.when(takes_right & jnp.logical_not(by_last))
            def _():
                pass_left(c)

            @pl.when(end & (h == 0) & (c == block_count - 1))
            def _():
                def late(k, _):
                    @pl.when(first_end)
                    def _():
                        to_right(0, k).start()

                    @pl.when(last_end)
                    def _():
                        to_left(0, k).start()

                    return 0

                lax.fori_loop(0, block_count, late, 0)

            @pl.when(helper & (h == 0))
            def _():
                given(c).wait_recv()
                for d in range(1, owners):
                    across(d, c).start()
                beside(0, r, c).start()

            @pl.when(helper & (h * block_count + c >= 1) & (h * block_count + c <= block_count))
            def _():
                for d in range(1, owners):
                    from_across(d, h * block_count + c - 1).wait_recv()
                    beside(d, r, h * block_count + c - 1).start()

            at = pl.ds(pl.multiple_of(c * size, size), size)

            @pl.when(takes_left)
            def _():
                acc[at, :] += product(left_shard, c)

            @pl.when(takes_right)
            def _():
                acc[at, :] += product(right_shard, c)

            @pl.when(helper & (h == n - 3))
            def _():
                @pl.when(c == 0)
                def _():
                    def arrived(j, _):
                        for d in range(owners):
                            beside(d, 1 - r, j).wait_recv()
                        return 0

                    lax.fori_loop(0, block_count, arrived, 0)

                base = jnp.where(by_first, mid, 0)
                far_sum[...] = jnp.zeros_like(far_sum)

                def far(k, _):
                    far_sum[...] += jnp.dot(
                        g[base + k, at, :], wx[pl.ds(pl.multiple_of(k * feats, feats), feats), :],
                        preferred_element_type=jnp.float32,
                    )
                    return 0

                lax.fori_loop(0, n - mid, far, 0)
                aid_out[at, :] = far_sum[...].astype(jnp.bfloat16)
                aid(c, end_of).start()

            return 0

        lax.fori_loop(0, block_count, chunk, 0)

        @pl.when((z == h) & has_right)
        def _():
            @pl.when(has_left)
            def _():
                sum_right.wait_recv()

            snd_r[...] = part[...] + pre[...]
            sum_right.start()

        @pl.when((n - 1 - z == h) & has_left)
        def _():
            @pl.when(has_right)
            def _():
                sum_left.wait_recv()

            snd_l[...] = part[...] + suf[...]
            sum_left.start()

        return 0

    lax.fori_loop(0, n - 1, hop, 0)

    @pl.when(z == n - 1)
    def _():
        sum_right.wait_recv()

    @pl.when(z == 0)
    def _():
        sum_left.wait_recv()

    for b in range(block_count):
        at = pl.ds(b * size, size)
        reduced = jnp.transpose(part[b] + pre[b] + suf[b]).astype(jnp.bfloat16)
        lora = jnp.dot(reduced, up[pos[b]], preferred_element_type=jnp.float32)

        @pl.when(end)
        def _():
            aid(b, helper_of).wait_recv()
            acc[at, :] += aid_in[at, :].astype(jnp.float32)

        out[at, :] = (acc[at, :] + lowrank_scale * lora).astype(jnp.bfloat16)

    def sent(h, _):
        def chunk(c, _):
            @pl.when(has_right & (z - h >= 0) & jnp.logical_not(by_last & (z - h < mid)))
            def _():
                to_right(h, c).wait_send()

            @pl.when(has_left & (z + h <= n - 1) & jnp.logical_not(by_first & (z + h >= mid)))
            def _():
                to_left(h, c).wait_send()

            return 0

        lax.fori_loop(0, block_count, chunk, 0)
        return 0

    lax.fori_loop(0, n - 1, sent, 0)
    give_w.wait_send()
    for gift in gives:
        gift.wait_send()

    def done(j, _):
        @pl.when(giver)
        def _():
            for core in range(2):
                give(core, j).wait_send()

        @pl.when(helper)
        def _():
            for d in range(1, owners):
                across(d, j).wait_send()
            for d in range(owners):
                beside(d, r, j).wait_send()
            aid(j, end_of).wait_send()

        return 0

    lax.fori_loop(0, block_count, done, 0)

    @pl.when(has_right)
    def _():
        sum_right.wait_send()

    @pl.when(has_left)
    def _():
        sum_left.wait_send()


def body(mesh, tokens, adapter_per_block, placement, weight, lowrank_down_weight, lowrank_up_weight):
    rows, feats = tokens.shape
    block_count = adapter_per_block.shape[0]
    size = rows // block_count
    slots, rank, _ = lowrank_down_weight.shape
    half, columns = weight.shape
    n, owners = mesh.shape["tp"], mesh.shape["ad"]
    per_owner = (block_count + owners - 1) // owners
    table = jnp.arange(placement.shape[0], dtype=jnp.int32)
    store_row = jnp.sum(
        jnp.where(adapter_per_block[:, None] == table[None, :], placement[None, :], 0), axis=1
    )
    owner_of = store_row // slots
    slot_of = store_row % slots
    index = jnp.arange(block_count, dtype=jnp.int32)
    earlier = (owner_of[:, None] == owner_of[None, :]) & (index[None, :] < index[:, None])
    position = owner_of * per_owner + jnp.sum(earlier.astype(jnp.int32), axis=1)
    places = jnp.arange(owners * per_owner, dtype=jnp.int32)
    asks = jnp.sum(jnp.where(position[None, :] == places[:, None], slot_of[None, :], 0), axis=1)
    asked = lax.all_to_all(
        asks.reshape(owners, per_owner), "ad", split_axis=0, concat_axis=0, tiled=True
    ).reshape(-1)
    down_pick = jnp.take(lowrank_down_weight, asked, axis=0, mode="clip")
    up_pick = jnp.take(lowrank_up_weight, asked, axis=0, mode="clip")
    total = owners * per_owner
    bf16, f32 = jnp.bfloat16, jnp.float32
    sums = pltpu.VMEM((block_count, rank, size), f32)
    anyspace = pl.BlockSpec(memory_space=pl.ANY)
    peers = max(owners - 1, 1)
    return pl.pallas_call(
        functools.partial(kernel, n, owners, block_count),
        out_shape=jax.ShapeDtypeStruct((rows, columns), bf16),
        in_specs=[pl.BlockSpec(memory_space=pltpu.SMEM)] + [anyspace] * 4,
        out_specs=pl.BlockSpec(memory_space=pltpu.VMEM),
        scratch_shapes=[
            pltpu.VMEM((n, rows, feats), bf16),
            pltpu.VMEM((2 * half, columns), bf16),
            pltpu.VMEM((rows, columns), f32),
            pltpu.VMEM((total, rank, feats), bf16),
            pltpu.VMEM((total, rank, columns), bf16),
            sums, sums, sums, sums, sums,
            pltpu.VMEM((half, columns), bf16),
            pltpu.VMEM((size, columns), f32),
            pltpu.VMEM((rows, columns), bf16),
            pltpu.VMEM((rows, columns), bf16),
            pltpu.SemaphoreType.DMA((4,)),
            pltpu.SemaphoreType.DMA((2, n - 1, block_count)),
            pltpu.SemaphoreType.DMA((2, n - 1, block_count)),
            pltpu.SemaphoreType.DMA,
            pltpu.SemaphoreType.DMA,
            pltpu.SemaphoreType.DMA((2, peers)),
            pltpu.SemaphoreType.DMA((2, peers)),
            pltpu.SemaphoreType.DMA((2,)),
            pltpu.SemaphoreType.DMA((2,)),
            pltpu.SemaphoreType.DMA((2, block_count)),
            pltpu.SemaphoreType.DMA((block_count,)),
            pltpu.SemaphoreType.DMA((peers, block_count)),
            pltpu.SemaphoreType.DMA((peers, block_count)),
            pltpu.SemaphoreType.DMA((owners, block_count)),
            pltpu.SemaphoreType.DMA((owners, block_count)),
            pltpu.SemaphoreType.DMA((block_count,)),
            pltpu.SemaphoreType.DMA((block_count,)),
        ],
        compiler_params=pltpu.CompilerParams(
            collective_id=0, has_side_effects=True, vmem_limit_bytes=56 * 1024 * 1024
        ),
        cost_estimate=pl.CostEstimate(
            flops=4 * rows * half * columns, bytes_accessed=4 * half * columns, transcendentals=0
        ),
    )(position, tokens, weight, down_pick, up_pick)


def solution(mesh):
    return jax.shard_map(
        functools.partial(body, mesh),
        mesh=mesh,
        in_specs=(
            P(("groups", "ad", "rep"), "tp"),
            P(("groups", "ad", "rep")),
            P(),
            P("rep", "tp"),
            P("ad", None, "tp"),
            P("ad", None, "tp"),
        ),
        out_specs=P(("groups", "ad", "rep"), "tp"),
        check_vma=False,
    )
```

```python
import functools

import jax
import jax.numpy as jnp
from jax import lax
from jax.experimental import pallas as pl
from jax.experimental.pallas import tpu as pltpu
from jax.sharding import PartitionSpec as P

MESH = pl.DeviceIdType.MESH
lowrank_scale = 2.0
NT = (((1,), (1,)), ((), ()))


def remote(src, dst, send, recv, device):
    return pltpu.make_async_remote_copy(
        src_ref=src, dst_ref=dst, send_sem=send, recv_sem=recv, device_id=device, device_id_type=MESH
    )


def kernel(
    n, owners, crowd, block_count,
    pos, tok, wt, dpick, upick, out,
    g, w, acc, dn, up, part, pre, suf, snd_r, snd_l, wx, far_sum, aid_out, aid_in,
    local, tok_send, tok_recv, w_send, w_recv, a_send, a_recv, sum_send, sum_recv,
    gv_send, gv_recv, x_send, x_recv, p_send, p_recv, aid_send, aid_recv,
):
    z, a, r = lax.axis_index("tp"), lax.axis_index("ad"), lax.axis_index("rep")
    me = lax.axis_index("groups") * owners + a
    rows, feats = tok.shape
    half = wt.shape[0]
    size = rows // block_count
    per = dpick.shape[0] // owners
    has_left, has_right = z > 0, z < n - 1
    mid = n // 2
    first_end, last_end, by_first, by_last = z == 0, z == n - 1, z == 1, z == n - 2
    end, helper = first_end | last_end, by_first | by_last
    end_of, helper_of = jnp.where(by_first, 0, n - 1), jnp.where(first_end, 1, n - 2)
    giver = (first_end & (r == 1)) | (last_end & (r == 0))
    sub = half // (2 * crowd * block_count)

    def peer(t):
        return {"groups": t // owners, "ad": lax.rem(t, owners)}


    own_tok = pltpu.make_async_copy(tok, g.at[z], local.at[0])
    own_w = pltpu.make_async_copy(wt, w.at[pl.ds(r * half, half)], local.at[1])
    own_dn = pltpu.make_async_copy(dpick.at[pl.ds(a * per, per)], dn.at[pl.ds(a * per, per)], local.at[2])
    own_up = pltpu.make_async_copy(upick.at[pl.ds(a * per, per)], up.at[pl.ds(a * per, per)], local.at[3])
    own_tok.start()

    barrier = pltpu.get_barrier_semaphore()

    @pl.when(has_left)
    def _():
        for core in range(2):
            pl.semaphore_signal(barrier, inc=1, device_id={"tp": z - 1, "rep": core}, device_id_type=MESH)

    @pl.when(has_right)
    def _():
        for core in range(2):
            pl.semaphore_signal(barrier, inc=1, device_id={"tp": z + 1, "rep": core}, device_id_type=MESH)

    pl.semaphore_signal(barrier, inc=1, device_id={"rep": 1 - r}, device_id_type=MESH)
    for d in range(1, crowd):
        pl.semaphore_signal(barrier, inc=1, device_id=peer(lax.rem(me + d, crowd)), device_id_type=MESH)
    own_tok.wait()
    pl.semaphore_wait(
        barrier, crowd + jnp.where(has_left, 2, 0) + jnp.where(has_right, 2, 0)
    )

    def piece(shard, c):
        return g.at[shard, pl.ds(pl.multiple_of(c * size, size), size)]

    def to_right(h, c):
        return remote(piece(z - h, c), piece(z - h, c), tok_send.at[0, h, c], tok_recv.at[0, h, c], {"tp": z + 1})

    def to_left(h, c):
        return remote(piece(z + h, c), piece(z + h, c), tok_send.at[1, h, c], tok_recv.at[1, h, c], {"tp": z - 1})

    def from_left(h, c):
        return remote(piece(z - 1 - h, c), piece(z - 1 - h, c), tok_send.at[0, h, c], tok_recv.at[0, h, c], {"tp": z - 1})

    def from_right(h, c):
        return remote(piece(z + 1 + h, c), piece(z + 1 + h, c), tok_send.at[1, h, c], tok_recv.at[1, h, c], {"tp": z + 1})

    def share(owner, core, j):
        return pl.ds(pl.multiple_of(((owner * 2 + core) * block_count + j) * sub, sub), sub)

    def give(core, j):
        at = share(me, core, j)
        return remote(wt.at[at], wx.at[at], gv_send.at[core, j], gv_recv.at[j], {"tp": helper_of, "rep": core})

    def given(j):
        at = share(me, r, j)
        return remote(wt.at[at], wx.at[at], gv_send.at[0, j], gv_recv.at[j], {"tp": end_of})

    def across(d, j):
        at = wx.at[share(me, r, j)]
        return remote(at, at, x_send.at[d - 1, j], x_recv.at[d - 1, j], peer(lax.rem(me + d, crowd)))

    def from_across(d, j):
        at = wx.at[share(lax.rem(me + crowd - d, crowd), r, j)]
        return remote(at, at, x_send.at[d - 1, j], x_recv.at[d - 1, j], peer(lax.rem(me + crowd - d, crowd)))

    def beside(d, core, j):
        at = wx.at[share(lax.rem(me + crowd - d, crowd), core, j)]
        return remote(at, at, p_send.at[d, j], p_recv.at[d, j], {"rep": 1 - r})

    def aid(c, device):
        at = pl.ds(pl.multiple_of(c * size, size), size)
        return remote(aid_out.at[at], aid_in.at[at], aid_send.at[c], aid_recv.at[c], {"tp": device})

    @pl.when(giver)
    def _():
        def start(j, _):
            for core in range(2):
                give(core, j).start()
            return 0

        lax.fori_loop(0, block_count, start, 0)

    def first(c, _):
        @pl.when(has_left & jnp.logical_not(last_end))
        def _():
            to_left(0, c).start()

        @pl.when(has_right & jnp.logical_not(first_end))
        def _():
            to_right(0, c).start()

        return 0

    lax.fori_loop(0, block_count, first, 0)

    give_w = remote(wt, w.at[pl.ds(r * half, half)], w_send, w_recv, {"rep": 1 - r})
    take_w = remote(wt, w.at[pl.ds((1 - r) * half, half)], w_send, w_recv, {"rep": 1 - r})
    give_w.start()
    own_w.start()
    own_dn.start()
    own_up.start()
    gives, takes = [], []
    for d in range(1, owners):
        to, frm = lax.rem(a + d, owners), lax.rem(a + owners - d, owners)
        for k, (pick, store) in enumerate(((dpick, dn), (upick, up))):
            gives.append(remote(
                pick.at[pl.ds(to * per, per)], store.at[pl.ds(a * per, per)],
                a_send.at[k, d - 1], a_recv.at[k, d - 1], {"ad": to},
            ))
            takes.append(remote(
                pick.at[pl.ds(to * per, per)], store.at[pl.ds(frm * per, per)],
                a_send.at[k, d - 1], a_recv.at[k, d - 1], {"ad": frm},
            ))
            gives[-1].start()

    @pl.when(z == 0)
    def _():
        pre[...] = jnp.zeros_like(pre)

    @pl.when(z == n - 1)
    def _():
        suf[...] = jnp.zeros_like(suf)

    def product(shard, c):
        at = pl.ds(pl.multiple_of(c * size, size), size)
        return jnp.dot(
            g[shard, at, :], w[pl.ds(pl.multiple_of(shard * feats, feats), feats), :],
            preferred_element_type=jnp.float32,
        )

    own_w.wait()
    take_w.wait_recv()

    def own(c, _):
        acc[pl.ds(pl.multiple_of(c * size, size), size), :] = product(z, c)
        return 0

    lax.fori_loop(0, block_count, own, 0)

    own_dn.wait()
    own_up.wait()
    for take in takes:
        take.wait_recv()
    for b in range(block_count):
        part[b] = lax.dot_general(
            dn[pos[b]], g[z, pl.ds(b * size, size), :], NT, preferred_element_type=jnp.float32
        )

    sum_right = remote(snd_r, pre, sum_send.at[0], sum_recv.at[0], {"tp": z + 1})
    sum_left = remote(snd_l, suf, sum_send.at[1], sum_recv.at[1], {"tp": z - 1})

    def hop(h, _):
        hr = h - jnp.where(by_first, 1, 0)
        hl = h - jnp.where(by_last, 1, 0)
        left_shard, right_shard = z - 1 - hr, z + 1 + hl
        takes_left = (hr >= 0) & (left_shard >= 0) & jnp.logical_not(last_end & (left_shard < mid))
        takes_right = (hl >= 0) & (right_shard <= n - 1) & jnp.logical_not(first_end & (right_shard >= mid))

        def pass_right(c, _=0):
            from_left(hr, c).wait_recv()

            @pl.when(has_right & jnp.logical_not(by_last & (left_shard < mid)))
            def _():
                to_right(hr + 1, c).start()

            return 0

        def pass_left(c, _=0):
            from_right(hl, c).wait_recv()

            @pl.when(has_left & jnp.logical_not(by_first & (right_shard >= mid)))
            def _():
                to_left(hl + 1, c).start()

            return 0

        def chunk(c, _):
            low = jnp.where(c == 0, 0, c + 1)
            high = jnp.where(c + 2 < block_count, c + 2, block_count)

            @pl.when(takes_left & by_first)
            def _():
                lax.fori_loop(low, high, pass_right, 0)

            @pl.when(takes_right & by_last)
            def _():
                lax.fori_loop(low, high, pass_left, 0)

            @pl.when(takes_left & jnp.logical_not(by_first))
            def _():
                pass_right(c)

            @pl.when(takes_right & jnp.logical_not(by_last))
            def _():
                pass_left(c)

            @pl.when(end & (h == 0) & (c == (block_count - 1) // 2))
            def _():
                def late(k, _):
                    @pl.when(first_end)
                    def _():
                        to_right(0, k).start()

                    @pl.when(last_end)
                    def _():
                        to_left(0, k).start()

                    return 0

                lax.fori_loop(0, block_count, late, 0)

            @pl.when(helper & (h == 0))
            def _():
                given(c).wait_recv()
                for d in range(1, crowd):
                    across(d, c).start()
                beside(0, r, c).start()

            @pl.when(helper & (h * block_count + c >= 1) & (h * block_count + c <= block_count))
            def _():
                for d in range(1, crowd):
                    from_across(d, h * block_count + c - 1).wait_recv()
                    beside(d, r, h * block_count + c - 1).start()

            at = pl.ds(pl.multiple_of(c * size, size), size)

            @pl.when(takes_left)
            def _():
                acc[at, :] += product(left_shard, c)

            @pl.when(takes_right)
            def _():
                acc[at, :] += product(right_shard, c)

            @pl.when(helper & (h == n - 3))
            def _():
                @pl.when(c == 0)
                def _():
                    def arrived(j, _):
                        for d in range(crowd):
                            beside(d, 1 - r, j).wait_recv()
                        return 0

                    lax.fori_loop(0, block_count, arrived, 0)

                base = jnp.where(by_first, mid, 0)
                far_sum[...] = jnp.zeros_like(far_sum)

                def far(k, _):
                    far_sum[...] += jnp.dot(
                        g[base + k, at, :], wx[pl.ds(pl.multiple_of(k * feats, feats), feats), :],
                        preferred_element_type=jnp.float32,
                    )
                    return 0

                lax.fori_loop(0, n - mid, far, 0)
                aid_out[at, :] = far_sum[...].astype(jnp.bfloat16)
                aid(c, end_of).start()

            return 0

        lax.fori_loop(0, block_count, chunk, 0)

        @pl.when((z == h) & has_right)
        def _():
            @pl.when(has_left)
            def _():
                sum_right.wait_recv()

            snd_r[...] = part[...] + pre[...]
            sum_right.start()

        @pl.when((n - 1 - z == h) & has_left)
        def _():
            @pl.when(has_right)
            def _():
                sum_left.wait_recv()

            snd_l[...] = part[...] + suf[...]
            sum_left.start()

        return 0

    lax.fori_loop(0, n - 1, hop, 0)

    @pl.when(z == n - 1)
    def _():
        sum_right.wait_recv()

    @pl.when(z == 0)
    def _():
        sum_left.wait_recv()

    for b in range(block_count):
        at = pl.ds(b * size, size)
        reduced = jnp.transpose(part[b] + pre[b] + suf[b]).astype(jnp.bfloat16)
        lora = jnp.dot(reduced, up[pos[b]], preferred_element_type=jnp.float32)

        @pl.when(end)
        def _():
            aid(b, helper_of).wait_recv()
            acc[at, :] += aid_in[at, :].astype(jnp.float32)

        out[at, :] = (acc[at, :] + lowrank_scale * lora).astype(jnp.bfloat16)

    def sent(h, _):
        def chunk(c, _):
            @pl.when(has_right & (z - h >= 0) & jnp.logical_not(by_last & (z - h < mid)))
            def _():
                to_right(h, c).wait_send()

            @pl.when(has_left & (z + h <= n - 1) & jnp.logical_not(by_first & (z + h >= mid)))
            def _():
                to_left(h, c).wait_send()

            return 0

        lax.fori_loop(0, block_count, chunk, 0)
        return 0

    lax.fori_loop(0, n - 1, sent, 0)
    give_w.wait_send()
    for gift in gives:
        gift.wait_send()

    def done(j, _):
        @pl.when(giver)
        def _():
            for core in range(2):
                give(core, j).wait_send()

        @pl.when(helper)
        def _():
            for d in range(1, crowd):
                across(d, j).wait_send()
            for d in range(crowd):
                beside(d, r, j).wait_send()
            aid(j, end_of).wait_send()

        return 0

    lax.fori_loop(0, block_count, done, 0)

    @pl.when(has_right)
    def _():
        sum_right.wait_send()

    @pl.when(has_left)
    def _():
        sum_left.wait_send()


def body(mesh, tokens, adapter_per_block, placement, weight, lowrank_down_weight, lowrank_up_weight):
    rows, feats = tokens.shape
    block_count = adapter_per_block.shape[0]
    size = rows // block_count
    slots, rank, _ = lowrank_down_weight.shape
    half, columns = weight.shape
    n, owners = mesh.shape["tp"], mesh.shape["ad"]
    crowd = mesh.shape["groups"] * owners
    per_owner = (block_count + owners - 1) // owners
    table = jnp.arange(placement.shape[0], dtype=jnp.int32)
    store_row = jnp.sum(
        jnp.where(adapter_per_block[:, None] == table[None, :], placement[None, :], 0), axis=1
    )
    owner_of = store_row // slots
    slot_of = store_row % slots
    index = jnp.arange(block_count, dtype=jnp.int32)
    earlier = (owner_of[:, None] == owner_of[None, :]) & (index[None, :] < index[:, None])
    position = owner_of * per_owner + jnp.sum(earlier.astype(jnp.int32), axis=1)
    places = jnp.arange(owners * per_owner, dtype=jnp.int32)
    asks = jnp.sum(jnp.where(position[None, :] == places[:, None], slot_of[None, :], 0), axis=1)
    asked = lax.all_to_all(
        asks.reshape(owners, per_owner), "ad", split_axis=0, concat_axis=0, tiled=True
    ).reshape(-1)
    down_pick = jnp.take(lowrank_down_weight, asked, axis=0, mode="clip")
    up_pick = jnp.take(lowrank_up_weight, asked, axis=0, mode="clip")
    total = owners * per_owner
    bf16, f32 = jnp.bfloat16, jnp.float32
    sums = pltpu.VMEM((block_count, rank, size), f32)
    anyspace = pl.BlockSpec(memory_space=pl.ANY)
    peers = max(owners - 1, 1)
    return pl.pallas_call(
        functools.partial(kernel, n, owners, crowd, block_count),
        out_shape=jax.ShapeDtypeStruct((rows, columns), bf16),
        in_specs=[pl.BlockSpec(memory_space=pltpu.SMEM)] + [anyspace] * 4,
        out_specs=pl.BlockSpec(memory_space=pltpu.VMEM),
        scratch_shapes=[
            pltpu.VMEM((n, rows, feats), bf16),
            pltpu.VMEM((2 * half, columns), bf16),
            pltpu.VMEM((rows, columns), f32),
            pltpu.VMEM((total, rank, feats), bf16),
            pltpu.VMEM((total, rank, columns), bf16),
            sums, sums, sums, sums, sums,
            pltpu.VMEM((half, columns), bf16),
            pltpu.VMEM((size, columns), f32),
            pltpu.VMEM((rows, columns), bf16),
            pltpu.VMEM((rows, columns), bf16),
            pltpu.SemaphoreType.DMA((4,)),
            pltpu.SemaphoreType.DMA((2, n - 1, block_count)),
            pltpu.SemaphoreType.DMA((2, n - 1, block_count)),
            pltpu.SemaphoreType.DMA,
            pltpu.SemaphoreType.DMA,
            pltpu.SemaphoreType.DMA((2, peers)),
            pltpu.SemaphoreType.DMA((2, peers)),
            pltpu.SemaphoreType.DMA((2,)),
            pltpu.SemaphoreType.DMA((2,)),
            pltpu.SemaphoreType.DMA((2, block_count)),
            pltpu.SemaphoreType.DMA((block_count,)),
            pltpu.SemaphoreType.DMA((crowd - 1, block_count)),
            pltpu.SemaphoreType.DMA((crowd - 1, block_count)),
            pltpu.SemaphoreType.DMA((crowd, block_count)),
            pltpu.SemaphoreType.DMA((crowd, block_count)),
            pltpu.SemaphoreType.DMA((block_count,)),
            pltpu.SemaphoreType.DMA((block_count,)),
        ],
        compiler_params=pltpu.CompilerParams(
            collective_id=0, has_side_effects=True, vmem_limit_bytes=56 * 1024 * 1024
        ),
        cost_estimate=pl.CostEstimate(
            flops=4 * rows * half * columns, bytes_accessed=4 * half * columns, transcendentals=0
        ),
    )(position, tokens, weight, down_pick, up_pick)


def solution(mesh):
    return jax.shard_map(
        functools.partial(body, mesh),
        mesh=mesh,
        in_specs=(
            P(("groups", "ad", "rep"), "tp"),
            P(("groups", "ad", "rep")),
            P(),
            P("rep", "tp"),
            P("ad", None, "tp"),
            P("ad", None, "tp"),
        ),
        out_specs=P(("groups", "ad", "rep"), "tp"),
        check_vma=False,
    )
```

```python
import functools

import jax
import jax.numpy as jnp
from jax import lax
from jax.experimental import pallas as pl
from jax.experimental.pallas import tpu as pltpu
from jax.sharding import PartitionSpec as P

MESH = pl.DeviceIdType.MESH
lowrank_scale = 2.0
NT = (((1,), (1,)), ((), ()))


def remote(src, dst, send, recv, device):
    return pltpu.make_async_remote_copy(
        src_ref=src, dst_ref=dst, send_sem=send, recv_sem=recv, device_id=device, device_id_type=MESH
    )


def kernel(
    n, owners, crowd, block_count,
    pos, tok, wt, dpick, upick, out,
    g, w, acc, dn, up, part, pre, suf, snd_r, snd_l, wx, far_sum, aid_out, aid_in,
    local, tok_send, tok_recv, w_send, w_recv, a_send, a_recv, sum_send, sum_recv,
    gv_send, gv_recv, x_send, x_recv, p_send, p_recv, aid_send, aid_recv,
):
    z, a, r = lax.axis_index("tp"), lax.axis_index("ad"), lax.axis_index("rep")
    me = lax.axis_index("groups") * owners + a
    rows, feats = tok.shape
    half = wt.shape[0]
    size = rows // block_count
    per = dpick.shape[0] // owners
    has_left, has_right = z > 0, z < n - 1
    mid = n // 2
    first_end, last_end, by_first, by_last = z == 0, z == n - 1, z == 1, z == n - 2
    end, helper = first_end | last_end, by_first | by_last
    end_of, helper_of = jnp.where(by_first, 0, n - 1), jnp.where(first_end, 1, n - 2)
    giver = (first_end & (r == 1)) | (last_end & (r == 0))
    sub = half // (2 * crowd * block_count)

    def peer(t):
        return {"groups": t // owners, "ad": lax.rem(t, owners)}


    own_tok = pltpu.make_async_copy(tok, g.at[z], local.at[0])
    own_w = pltpu.make_async_copy(wt, w.at[pl.ds(r * half, half)], local.at[1])
    own_dn = pltpu.make_async_copy(dpick.at[pl.ds(a * per, per)], dn.at[pl.ds(a * per, per)], local.at[2])
    own_up = pltpu.make_async_copy(upick.at[pl.ds(a * per, per)], up.at[pl.ds(a * per, per)], local.at[3])
    own_tok.start()

    barrier = pltpu.get_barrier_semaphore()

    @pl.when(has_left)
    def _():
        for core in range(2):
            pl.semaphore_signal(barrier, inc=1, device_id={"tp": z - 1, "rep": core}, device_id_type=MESH)

    @pl.when(has_right)
    def _():
        for core in range(2):
            pl.semaphore_signal(barrier, inc=1, device_id={"tp": z + 1, "rep": core}, device_id_type=MESH)

    pl.semaphore_signal(barrier, inc=1, device_id={"rep": 1 - r}, device_id_type=MESH)
    for d in range(1, crowd):
        pl.semaphore_signal(barrier, inc=1, device_id=peer(lax.rem(me + d, crowd)), device_id_type=MESH)
    own_tok.wait()
    pl.semaphore_wait(
        barrier, crowd + jnp.where(has_left, 2, 0) + jnp.where(has_right, 2, 0)
    )

    def piece(shard, c):
        return g.at[shard, pl.ds(pl.multiple_of(c * size, size), size)]

    def to_right(h, c):
        return remote(piece(z - h, c), piece(z - h, c), tok_send.at[0, h, c], tok_recv.at[0, h, c], {"tp": z + 1})

    def to_left(h, c):
        return remote(piece(z + h, c), piece(z + h, c), tok_send.at[1, h, c], tok_recv.at[1, h, c], {"tp": z - 1})

    def from_left(h, c):
        return remote(piece(z - 1 - h, c), piece(z - 1 - h, c), tok_send.at[0, h, c], tok_recv.at[0, h, c], {"tp": z - 1})

    def from_right(h, c):
        return remote(piece(z + 1 + h, c), piece(z + 1 + h, c), tok_send.at[1, h, c], tok_recv.at[1, h, c], {"tp": z + 1})

    def share(owner, core, j):
        return pl.ds(pl.multiple_of(((owner * 2 + core) * block_count + j) * sub, sub), sub)

    def give(core, j):
        at = share(me, core, j)
        return remote(wt.at[at], wx.at[at], gv_send.at[core, j], gv_recv.at[j], {"tp": helper_of, "rep": core})

    def given(j):
        at = share(me, r, j)
        return remote(wt.at[at], wx.at[at], gv_send.at[0, j], gv_recv.at[j], {"tp": end_of})

    def across(d, j):
        at = wx.at[share(me, r, j)]
        return remote(at, at, x_send.at[d - 1, j], x_recv.at[d - 1, j], peer(lax.rem(me + d, crowd)))

    def from_across(d, j):
        at = wx.at[share(lax.rem(me + crowd - d, crowd), r, j)]
        return remote(at, at, x_send.at[d - 1, j], x_recv.at[d - 1, j], peer(lax.rem(me + crowd - d, crowd)))

    def beside(d, core, j):
        at = wx.at[share(lax.rem(me + crowd - d, crowd), core, j)]
        return remote(at, at, p_send.at[d, j], p_recv.at[d, j], {"rep": 1 - r})

    def aid(c, device):
        at = pl.ds(pl.multiple_of(c * size, size), size)
        return remote(aid_out.at[at], aid_in.at[at], aid_send.at[c], aid_recv.at[c], {"tp": device})

    @pl.when(giver)
    def _():
        def start(j, _):
            for core in range(2):
                give(core, j).start()
            return 0

        lax.fori_loop(0, block_count, start, 0)

    def first(c, _):
        @pl.when(has_left & jnp.logical_not(last_end))
        def _():
            to_left(0, c).start()

        @pl.when(has_right & jnp.logical_not(first_end))
        def _():
            to_right(0, c).start()

        return 0

    lax.fori_loop(0, block_count, first, 0)

    give_w = remote(wt, w.at[pl.ds(r * half, half)], w_send, w_recv, {"rep": 1 - r})
    take_w = remote(wt, w.at[pl.ds((1 - r) * half, half)], w_send, w_recv, {"rep": 1 - r})
    give_w.start()
    own_w.start()
    own_dn.start()
    own_up.start()
    gives, takes = [], []
    for d in range(1, owners):
        to, frm = lax.rem(a + d, owners), lax.rem(a + owners - d, owners)
        for k, (pick, store) in enumerate(((dpick, dn), (upick, up))):
            gives.append(remote(
                pick.at[pl.ds(to * per, per)], store.at[pl.ds(a * per, per)],
                a_send.at[k, d - 1], a_recv.at[k, d - 1], {"ad": to},
            ))
            takes.append(remote(
                pick.at[pl.ds(to * per, per)], store.at[pl.ds(frm * per, per)],
                a_send.at[k, d - 1], a_recv.at[k, d - 1], {"ad": frm},
            ))
            gives[-1].start()

    @pl.when(z == 0)
    def _():
        pre[...] = jnp.zeros_like(pre)

    @pl.when(z == n - 1)
    def _():
        suf[...] = jnp.zeros_like(suf)

    many = 2 if block_count % 2 == 0 else 1

    def group(c):
        return pl.ds(pl.multiple_of((c - (many - 1)) * size, size), many * size)

    def product(shard, at):
        return jnp.dot(
            g[shard, at, :], w[pl.ds(pl.multiple_of(shard * feats, feats), feats), :],
            preferred_element_type=jnp.float32,
        )

    own_w.wait()
    take_w.wait_recv()

    def own(c, _):
        at = group(c * many + many - 1)
        acc[at, :] = product(z, at)
        return 0

    lax.fori_loop(0, block_count // many, own, 0)

    own_dn.wait()
    own_up.wait()
    for take in takes:
        take.wait_recv()
    for b in range(block_count):
        part[b] = lax.dot_general(
            dn[pos[b]], g[z, pl.ds(b * size, size), :], NT, preferred_element_type=jnp.float32
        )

    sum_right = remote(snd_r, pre, sum_send.at[0], sum_recv.at[0], {"tp": z + 1})
    sum_left = remote(snd_l, suf, sum_send.at[1], sum_recv.at[1], {"tp": z - 1})

    def hop(h, _):
        hr = h - jnp.where(by_first, 1, 0)
        hl = h - jnp.where(by_last, 1, 0)
        left_shard, right_shard = z - 1 - hr, z + 1 + hl
        takes_left = (hr >= 0) & (left_shard >= 0) & jnp.logical_not(last_end & (left_shard < mid))
        takes_right = (hl >= 0) & (right_shard <= n - 1) & jnp.logical_not(first_end & (right_shard >= mid))

        def pass_right(c, _=0):
            from_left(hr, c).wait_recv()

            @pl.when(has_right & jnp.logical_not(by_last & (left_shard < mid)))
            def _():
                to_right(hr + 1, c).start()

            return 0

        def pass_left(c, _=0):
            from_right(hl, c).wait_recv()

            @pl.when(has_left & jnp.logical_not(by_first & (right_shard >= mid)))
            def _():
                to_left(hl + 1, c).start()

            return 0

        def chunk(c, _):
            low = jnp.where(c == 0, 0, c + 1)
            high = jnp.where(c + 2 < block_count, c + 2, block_count)

            @pl.when(takes_left & by_first)
            def _():
                lax.fori_loop(low, high, pass_right, 0)

            @pl.when(takes_right & by_last)
            def _():
                lax.fori_loop(low, high, pass_left, 0)

            @pl.when(takes_left & jnp.logical_not(by_first))
            def _():
                pass_right(c)

            @pl.when(takes_right & jnp.logical_not(by_last))
            def _():
                pass_left(c)

            @pl.when(end & (h == 0) & (c == (block_count - 1) // 2))
            def _():
                def late(k, _):
                    @pl.when(first_end)
                    def _():
                        to_right(0, k).start()

                    @pl.when(last_end)
                    def _():
                        to_left(0, k).start()

                    return 0

                lax.fori_loop(0, block_count, late, 0)

            @pl.when(helper & (h == 0))
            def _():
                given(c).wait_recv()
                for d in range(1, crowd):
                    across(d, c).start()
                beside(0, r, c).start()

            @pl.when(helper & (h * block_count + c >= 1) & (h * block_count + c <= block_count))
            def _():
                for d in range(1, crowd):
                    from_across(d, h * block_count + c - 1).wait_recv()
                    beside(d, r, h * block_count + c - 1).start()

            at = group(jnp.where(c < many - 1, many - 1, c))
            whole = lax.rem(c, many) == many - 1

            @pl.when(takes_left & whole)
            def _():
                acc[at, :] += product(left_shard, at)

            @pl.when(takes_right & whole)
            def _():
                acc[at, :] += product(right_shard, at)

            @pl.when(helper & (h == n - 3) & whole)
            def _():
                @pl.when(c == many - 1)
                def _():
                    def arrived(j, _):
                        for d in range(crowd):
                            beside(d, 1 - r, j).wait_recv()
                        return 0

                    lax.fori_loop(0, block_count, arrived, 0)

                base = jnp.where(by_first, mid, 0)
                far_sum[...] = jnp.zeros_like(far_sum)

                def far(k, _):
                    far_sum[...] += jnp.dot(
                        g[base + k, at, :], wx[pl.ds(pl.multiple_of(k * feats, feats), feats), :],
                        preferred_element_type=jnp.float32,
                    )
                    return 0

                lax.fori_loop(0, n - mid, far, 0)
                aid_out[at, :] = far_sum[...].astype(jnp.bfloat16)
                for k in range(many):
                    aid(c - (many - 1) + k, end_of).start()

            return 0

        lax.fori_loop(0, block_count, chunk, 0)

        @pl.when((z == h) & has_right)
        def _():
            @pl.when(has_left)
            def _():
                sum_right.wait_recv()

            snd_r[...] = part[...] + pre[...]
            sum_right.start()

        @pl.when((n - 1 - z == h) & has_left)
        def _():
            @pl.when(has_right)
            def _():
                sum_left.wait_recv()

            snd_l[...] = part[...] + suf[...]
            sum_left.start()

        return 0

    lax.fori_loop(0, n - 1, hop, 0)

    @pl.when(z == n - 1)
    def _():
        sum_right.wait_recv()

    @pl.when(z == 0)
    def _():
        sum_left.wait_recv()

    for b in range(block_count):
        at = pl.ds(b * size, size)
        reduced = jnp.transpose(part[b] + pre[b] + suf[b]).astype(jnp.bfloat16)
        lora = jnp.dot(reduced, up[pos[b]], preferred_element_type=jnp.float32)

        @pl.when(end)
        def _():
            aid(b, helper_of).wait_recv()
            acc[at, :] += aid_in[at, :].astype(jnp.float32)

        out[at, :] = (acc[at, :] + lowrank_scale * lora).astype(jnp.bfloat16)

    def sent(h, _):
        def chunk(c, _):
            @pl.when(has_right & (z - h >= 0) & jnp.logical_not(by_last & (z - h < mid)))
            def _():
                to_right(h, c).wait_send()

            @pl.when(has_left & (z + h <= n - 1) & jnp.logical_not(by_first & (z + h >= mid)))
            def _():
                to_left(h, c).wait_send()

            return 0

        lax.fori_loop(0, block_count, chunk, 0)
        return 0

    lax.fori_loop(0, n - 1, sent, 0)
    give_w.wait_send()
    for gift in gives:
        gift.wait_send()

    def done(j, _):
        @pl.when(giver)
        def _():
            for core in range(2):
                give(core, j).wait_send()

        @pl.when(helper)
        def _():
            for d in range(1, crowd):
                across(d, j).wait_send()
            for d in range(crowd):
                beside(d, r, j).wait_send()
            aid(j, end_of).wait_send()

        return 0

    lax.fori_loop(0, block_count, done, 0)

    @pl.when(has_right)
    def _():
        sum_right.wait_send()

    @pl.when(has_left)
    def _():
        sum_left.wait_send()


def body(mesh, tokens, adapter_per_block, placement, weight, lowrank_down_weight, lowrank_up_weight):
    rows, feats = tokens.shape
    block_count = adapter_per_block.shape[0]
    size = rows // block_count
    slots, rank, _ = lowrank_down_weight.shape
    half, columns = weight.shape
    n, owners = mesh.shape["tp"], mesh.shape["ad"]
    crowd = mesh.shape["groups"] * owners
    per_owner = (block_count + owners - 1) // owners
    table = jnp.arange(placement.shape[0], dtype=jnp.int32)
    store_row = jnp.sum(
        jnp.where(adapter_per_block[:, None] == table[None, :], placement[None, :], 0), axis=1
    )
    owner_of = store_row // slots
    slot_of = store_row % slots
    index = jnp.arange(block_count, dtype=jnp.int32)
    earlier = (owner_of[:, None] == owner_of[None, :]) & (index[None, :] < index[:, None])
    position = owner_of * per_owner + jnp.sum(earlier.astype(jnp.int32), axis=1)
    places = jnp.arange(owners * per_owner, dtype=jnp.int32)
    asks = jnp.sum(jnp.where(position[None, :] == places[:, None], slot_of[None, :], 0), axis=1)
    asked = lax.all_to_all(
        asks.reshape(owners, per_owner), "ad", split_axis=0, concat_axis=0, tiled=True
    ).reshape(-1)
    down_pick = jnp.take(lowrank_down_weight, asked, axis=0, mode="clip")
    up_pick = jnp.take(lowrank_up_weight, asked, axis=0, mode="clip")
    total = owners * per_owner
    bf16, f32 = jnp.bfloat16, jnp.float32
    sums = pltpu.VMEM((block_count, rank, size), f32)
    anyspace = pl.BlockSpec(memory_space=pl.ANY)
    peers = max(owners - 1, 1)
    return pl.pallas_call(
        functools.partial(kernel, n, owners, crowd, block_count),
        out_shape=jax.ShapeDtypeStruct((rows, columns), bf16),
        in_specs=[pl.BlockSpec(memory_space=pltpu.SMEM)] + [anyspace] * 4,
        out_specs=pl.BlockSpec(memory_space=pltpu.VMEM),
        scratch_shapes=[
            pltpu.VMEM((n, rows, feats), bf16),
            pltpu.VMEM((2 * half, columns), bf16),
            pltpu.VMEM((rows, columns), f32),
            pltpu.VMEM((total, rank, feats), bf16),
            pltpu.VMEM((total, rank, columns), bf16),
            sums, sums, sums, sums, sums,
            pltpu.VMEM((half, columns), bf16),
            pltpu.VMEM((size * (2 if block_count % 2 == 0 else 1), columns), f32),
            pltpu.VMEM((rows, columns), bf16),
            pltpu.VMEM((rows, columns), bf16),
            pltpu.SemaphoreType.DMA((4,)),
            pltpu.SemaphoreType.DMA((2, n - 1, block_count)),
            pltpu.SemaphoreType.DMA((2, n - 1, block_count)),
            pltpu.SemaphoreType.DMA,
            pltpu.SemaphoreType.DMA,
            pltpu.SemaphoreType.DMA((2, peers)),
            pltpu.SemaphoreType.DMA((2, peers)),
            pltpu.SemaphoreType.DMA((2,)),
            pltpu.SemaphoreType.DMA((2,)),
            pltpu.SemaphoreType.DMA((2, block_count)),
            pltpu.SemaphoreType.DMA((block_count,)),
            pltpu.SemaphoreType.DMA((crowd - 1, block_count)),
            pltpu.SemaphoreType.DMA((crowd - 1, block_count)),
            pltpu.SemaphoreType.DMA((crowd, block_count)),
            pltpu.SemaphoreType.DMA((crowd, block_count)),
            pltpu.SemaphoreType.DMA((block_count,)),
            pltpu.SemaphoreType.DMA((block_count,)),
        ],
        compiler_params=pltpu.CompilerParams(
            collective_id=0, has_side_effects=True, vmem_limit_bytes=56 * 1024 * 1024
        ),
        cost_estimate=pl.CostEstimate(
            flops=4 * rows * half * columns, bytes_accessed=4 * half * columns, transcendentals=0
        ),
    )(position, tokens, weight, down_pick, up_pick)


def solution(mesh):
    return jax.shard_map(
        functools.partial(body, mesh),
        mesh=mesh,
        in_specs=(
            P(("groups", "ad", "rep"), "tp"),
            P(("groups", "ad", "rep")),
            P(),
            P("rep", "tp"),
            P("ad", None, "tp"),
            P("ad", None, "tp"),
        ),
        out_specs=P(("groups", "ad", "rep"), "tp"),
        check_vma=False,
    )
```
